32 devices in a mesh: row: 4 (over z), col: 8 (over y, x, core).
Axes of the slice: x: 2, y: 2, z: 4, core: 2. Of those that a mesh axis runs over, the one named last changes fastest.
Arguments:
- right_side: bfloat16 [16384, 16384], P('row', 'col'), may hold values from -180 to 180
- theta_left: bfloat16 [512, 16384], P(None, 'row'), may hold values from -0.125 to 0.125
- theta_right: bfloat16 [512, 16384], P(None, 'col'), may hold values from -0.125 to 0.125
- query_rows: int32 [1024, 2], replicated, may hold values from 0 to 16384, as said below
- query_cols: int32 [1024, 2], replicated, may hold values from 0 to 16384, as said below
Outputs:
- residual: float32 [16384, 16384], P('row', 'col')
- step_ratio: float32 [1], replicated
- answers: float32 [1024], replicated
The draws below stay inside these ranges and needn't reach their ends.
Inputs may be any that keep to these rules, and one draw needn't show every extreme that they name: `query_rows`: each row is a start and an end with 0 <= start < end <= 16384. `query_cols`: each row is a start and an end with 0 <= start < end <= 16384.
All inputs are finite; a program needn't handle non-finite values.
Results may differ from the reference program's by a relative error of at most 0.0003.
Values sent between devices are 32-bit elements; how exact they have to be, the bound alone decides.
No kernel may reach another device: no remote copies, remote signals or barrier semaphores. Data moves between devices by JAX's collectives and lax.ppermute only.
A program may use at most 256 MiB of HBM per device.

```python
import jax
import jax.numpy as jnp
from jax import lax

NR = 16384
NC = 16384
P_SIZE = 512
NQ = 1024


def draw_right_side(key, part):
    noise_key, row_key, col_key = jax.random.split(key, 3)
    base_values = jnp.clip(jax.random.normal(noise_key, (NR, NC), jnp.float32), -6.0, 6.0)
    rise_factor = 3.0
    row_scale = jnp.exp(jax.random.uniform(row_key, (NR, 1), jnp.float32, -1.15, 1.15))
    col_scale = jnp.exp(jax.random.uniform(col_key, (1, NC), jnp.float32, -1.15, 1.15))
    row_trend = rise_factor ** (jnp.arange(NR, dtype=jnp.float32) / NR - 0.5)
    col_trend = 3.0 ** (jnp.arange(NC, dtype=jnp.float32) / NC - 0.5)
    return (base_values * row_scale * col_scale * row_trend[:, None] * col_trend[None, :]).astype(jnp.bfloat16)


def bounds_pair(key, extent):
    start_key, span_key = jax.random.split(key)
    starts = jax.random.randint(start_key, (NQ,), 0, extent)
    span_lengths = 1 + jax.random.randint(span_key, (NQ,), 0, extent) % (extent - starts)
    ends = (starts + span_lengths).at[0].set(extent)
    starts = starts.at[0].set(0)
    return jnp.stack([starts, ends], axis=1).astype(jnp.int32)


def draw_query_rows(key, part):
    return bounds_pair(jax.random.fold_in(key, 11), NR)


def draw_query_cols(key, part):
    return bounds_pair(jax.random.fold_in(key, 23), NC)


def level_of(stream_key, dims, cuts, smallest, top_value):
    gain = 1.0
    for axis_at, blocks in cuts:
        heights = jax.random.uniform(jax.random.fold_in(jax.random.fold_in(stream_key, 6), axis_at), (blocks,), jnp.float32, smallest / len(cuts), top_value / len(cuts))
        gain = gain * jnp.repeat(jnp.exp(heights), dims[axis_at] // blocks).reshape((-1,) + (1,) * (len(dims) - 1 - axis_at))
    return gain


def gaussian(rng, shape, width, reach, shards=(), kind=jnp.bfloat16):
    drawn = width * jax.random.normal(rng, shape, jnp.float32)
    if shards:
        drawn = drawn * level_of(rng, shape, shards, -0.22, 0.18)
    return jnp.clip(drawn, -reach, reach).astype(kind)


def setup_inputs(seed: int = 0) -> dict:
    key_of = jax.random.split(jax.random.key(seed), 6)
    return {
        "right_side": draw_right_side(jax.random.fold_in(key_of[5], 71), 0),
        "theta_left": gaussian(key_of[1], (P_SIZE, NR), (NR // 8) ** -0.5, 0.125, ((1, 4),)),
        "theta_right": gaussian(key_of[2], (P_SIZE, NC), (NC // 8) ** -0.5, 0.125, ((1, 8),)),
        "query_rows": draw_query_rows(jax.random.fold_in(key_of[5], 71), 0),
        "query_cols": draw_query_cols(jax.random.fold_in(key_of[5], 71), 0),
    }


def reference(right_side, theta_left, theta_right, query_rows, query_cols):
    highest = lax.Precision.HIGHEST
    start_field = right_side.astype(jnp.float32)
    left_wide = theta_left.astype(jnp.float32)
    right_wide = theta_right.astype(jnp.float32)
    summed_right = lax.dot_general(right_side, theta_right, (((1,), (1,)), ((), ())), preferred_element_type=jnp.float32)
    middle = start_field + jnp.dot(summed_right, right_wide, precision=highest, preferred_element_type=jnp.float32)
    summed_left = jnp.dot(left_wide, middle, precision=highest, preferred_element_type=jnp.float32)
    image_field = middle + lax.dot_general(left_wide, summed_left, (((0,), (0,)), ((), ())), precision=highest, preferred_element_type=jnp.float32)
    start_norm = jnp.sum(start_field * start_field)
    curvature = jnp.sum(start_field * image_field)
    alpha_step = start_norm / curvature
    residual = start_field - alpha_step * image_field
    step_ratio = (jnp.sum(residual * residual) / start_norm).reshape(1)
    solution = alpha_step * start_field
    prefix = jnp.cumsum(jnp.cumsum(solution, axis=1), axis=0)
    padded = jnp.pad(prefix, ((1, 0), (1, 0)))
    low_row = query_rows[:, 0]
    high_row = query_rows[:, 1]
    low_col = query_cols[:, 0]
    high_col = query_cols[:, 1]
    combined = padded[high_row, high_col] - padded[low_row, high_col] - padded[high_row, low_col] + padded[low_row, low_col]
    area = (high_row - low_row).astype(jnp.float32) * (high_col - low_col).astype(jnp.float32)
    answers = combined / jnp.sqrt(area)
    return (residual, step_ratio, answers)
```

```python
import functools

import jax
import jax.numpy as jnp
from jax import lax
from jax.experimental import pallas as pl
from jax.experimental.pallas import tpu as pltpu
from jax.sharding import PartitionSpec as P

F32 = jnp.float32
BF16 = jnp.bfloat16
VMEM_BYTES = 48 * 1024 * 1024


def params(sem_count):
    return pltpu.CompilerParams(
        dimension_semantics=("arbitrary",) * sem_count, vmem_limit_bytes=VMEM_BYTES
    )


def after(value, *earlier):
    return lax.optimization_barrier((value,) + earlier)[0]


def in_hbm(value):
    return pltpu.with_memory_space_constraint(value, pltpu.HBM)


def halves(value):
    high = value.astype(BF16)
    return high, (value - high.astype(F32)).astype(BF16)


def dot(a, b, dims=((1,), (0,))):
    return lax.dot_general(a, b, (dims, ((), ())), preferred_element_type=F32)


def rights_kernel(steps, x_ref, r_ref, l_ref, out_ref, core_ref):
    step = pl.program_id(0)
    summed = dot(x_ref[...], r_ref[...], ((1,), (1,)))
    out_ref[...] = summed.reshape(out_ref.shape)
    high, low = halves(summed)
    left = l_ref[...]
    part = dot(left, high) + dot(left, low)

    @pl.when(step == 0)
    def _():
        core_ref[...] = part

    @pl.when(step > 0)
    def _():
        core_ref[...] += part


def rights(x, r, l, groups, block):
    rows, cols = x.shape
    p = r.shape[0]
    each = rows // groups
    per_step = block // each
    return pl.pallas_call(
        functools.partial(rights_kernel, rows // block),
        out_shape=[
            jax.ShapeDtypeStruct((groups, each + p // groups, p), F32),
            jax.ShapeDtypeStruct((p, p), F32),
        ],
        grid=(rows // block,),
        in_specs=[
            pl.BlockSpec((block, cols), lambda i: (i, 0)),
            pl.BlockSpec((p, cols), lambda i: (0, 0)),
            pl.BlockSpec((p, block), lambda i: (0, i)),
        ],
        out_specs=[
            pl.BlockSpec((per_step, each, p), lambda i: (i, 0, 0)),
            pl.BlockSpec((p, p), lambda i: (0, 0)),
        ],
        compiler_params=params(1),
        cost_estimate=pl.CostEstimate(
            flops=4 * rows * cols * p, bytes_accessed=2 * rows * cols, transcendentals=0
        ),
        name="right_products",
    )(in_hbm(x), in_hbm(r), in_hbm(l))


def append_kernel(core_ref, old_ref, out_ref):
    out_ref[...] = core_ref[...]


def append_core(segments, core, each):
    groups, _, p = segments.shape
    share = p // groups
    return pl.pallas_call(
        append_kernel,
        out_shape=jax.ShapeDtypeStruct(segments.shape, F32),
        grid=(1,),
        in_specs=[
            pl.BlockSpec((groups, share, p), lambda i: (0, 0, 0)),
            pl.BlockSpec(memory_space=pl.ANY),
        ],
        out_specs=pl.BlockSpec((groups, share, p), lambda i: (0, each // share, 0)),
        input_output_aliases={1: 0},
        compiler_params=params(1),
        name="append_core",
    )(core.reshape(groups, share, p), segments)


def lefts_kernel(counts, l_ref, *refs):
    units = sum(counts)
    x_refs, out_refs = refs[:units], refs[units:]

    @pl.when(pl.program_id(0) == 0)
    def _():
        for out in out_refs:
            out[...] = jnp.zeros_like(out)

    left = l_ref[...]
    at = 0
    for count, out in zip(counts, out_refs):
        for k in range(count):
            width = x_refs[at].shape[1]
            out[:, k * width : (k + 1) * width] += dot(left, x_refs[at][...])
            at += 1


def lefts(l, x, start, counts, unit, block):
    p, rows = l.shape
    total = sum(counts)
    return pl.pallas_call(
        functools.partial(lefts_kernel, counts),
        out_shape=[jax.ShapeDtypeStruct((p, n * unit), F32) for n in counts],
        grid=(rows // block,),
        in_specs=[pl.BlockSpec((p, block), lambda i: (0, i))]
        + [
            pl.BlockSpec((block, unit), lambda i, u=start + u: (i, u)) for u in range(total)
        ],
        out_specs=[pl.BlockSpec((p, n * unit), lambda i: (0, 0)) for n in counts],
        compiler_params=params(1),
        cost_estimate=pl.CostEstimate(
            flops=2 * p * rows * total * unit,
            bytes_accessed=2 * rows * total * unit,
            transcendentals=0,
        ),
        name="left_products",
    )(in_hbm(l), *[in_hbm(x)] * total)


def mask_kernel(steps, col_start, rows_ref, cols_ref, x_ref, sums_ref, square_ref, acc):
    step = pl.program_id(0)
    block, width = x_ref.shape
    queries = acc.shape[0]

    @pl.when(step == 0)
    def _():
        acc[...] = jnp.zeros_like(acc)
        square_ref[...] = jnp.zeros_like(square_ref)

    values = x_ref[...]
    at = lax.broadcasted_iota(jnp.int32, (queries, block), 1) + step * block
    inside = (at >= rows_ref[:, 0:1]) & (at < rows_ref[:, 1:2])
    acc[...] += dot(inside.astype(F32).astype(BF16), values)
    wide = values.astype(F32)
    square_ref[...] += jnp.sum(wide * wide, axis=0, keepdims=True)

    @pl.when(step == steps - 1)
    def _():
        place = lax.broadcasted_iota(jnp.int32, (queries, width), 1) + col_start
        keep = (place >= cols_ref[:, 0:1]) & (place < cols_ref[:, 1:2])
        sums_ref[...] = jnp.sum(jnp.where(keep, acc[...], 0.0), axis=1, keepdims=True)


def mask_sums(x, row_bounds, col_bounds, start, width, block):
    rows = x.shape[0]
    queries = row_bounds.shape[0]
    steps = rows // block
    return pl.pallas_call(
        functools.partial(mask_kernel, steps, start),
        out_shape=[
            jax.ShapeDtypeStruct((queries, 1), F32),
            jax.ShapeDtypeStruct((1, width), F32),
        ],
        grid=(steps,),
        in_specs=[
            pl.BlockSpec((queries, 2), lambda i: (0, 0)),
            pl.BlockSpec((queries, 2), lambda i: (0, 0)),
            pl.BlockSpec((block, width), lambda i: (i, start // width)),
        ],
        out_specs=[
            pl.BlockSpec((queries, 1), lambda i: (0, 0)),
            pl.BlockSpec((1, width), lambda i: (0, 0)),
        ],
        scratch_shapes=[pltpu.VMEM((queries, width), F32)],
        compiler_params=params(1),
        cost_estimate=pl.CostEstimate(
            flops=2 * queries * rows * width, bytes_accessed=2 * rows * width, transcendentals=0
        ),
        name="interval_sums",
    )(row_bounds, col_bounds, in_hbm(x))


def finish_kernel(count, scale_ref, x_ref, s_ref, lt_ref, core_ref, r_ref, *refs):
    t_refs = refs[:count]
    out_ref, sum_ref, both, twice, both_low, twice_low = refs[count:]
    p, cols = r_ref.shape

    @pl.when(pl.program_id(0) == 0)
    def _():
        core_high, core_low = halves(core_ref[...])
        at = 0
        for t_ref in t_refs:
            span = slice(at, at + t_ref.shape[1])
            right = r_ref[:, span]
            high, low = halves(t_ref[...] + (dot(core_high, right) + dot(core_low, right)))
            twice[:p, span] = right
            twice[p:, span] = high
            twice_low[:p, span] = right
            twice_low[p:, span] = low
            at += t_ref.shape[1]
        sum_ref[...] = jnp.zeros_like(sum_ref)

    left = lt_ref[...]
    high, low = halves(s_ref[...])
    both[:, :p] = high
    both[:, p:] = left
    both_low[:, :p] = low
    both_low[:, p:] = left
    width = min(512, cols)
    for at in range(0, cols, width):
        span = slice(at, at + width)
        change = dot(both[...], twice[:, span]) + dot(both_low[...], twice_low[:, span])
        left_over = scale_ref[0] * x_ref[:, span].astype(F32) - scale_ref[1] * change
        out_ref[:, span] = left_over
        sum_ref[:, span] += jnp.sum(left_over * left_over, axis=0, keepdims=True)


def finish(scales, x, s, lt, core, r, parts, block):
    rows, cols = x.shape
    p = r.shape[0]
    whole = pl.BlockSpec(memory_space=pltpu.VMEM)
    return pl.pallas_call(
        functools.partial(finish_kernel, len(parts)),
        out_shape=[
            jax.ShapeDtypeStruct((rows, cols), F32),
            jax.ShapeDtypeStruct((1, cols), F32),
        ],
        grid=(rows // block,),
        in_specs=[
            pl.BlockSpec(memory_space=pltpu.SMEM),
            pl.BlockSpec((block, cols), lambda i: (i, 0)),
            pl.BlockSpec((block, p), lambda i: (i, 0)),
            pl.BlockSpec((block, p), lambda i: (i, 0)),
            whole,
            whole,
        ]
        + [whole] * len(parts),
        out_specs=[
            pl.BlockSpec((block, cols), lambda i: (i, 0)),
            pl.BlockSpec((1, cols), lambda i: (0, 0)),
        ],
        scratch_shapes=[
            pltpu.VMEM((block, 2 * p), BF16),
            pltpu.VMEM((2 * p, cols), BF16),
            pltpu.VMEM((block, 2 * p), BF16),
            pltpu.VMEM((2 * p, cols), BF16),
        ],
        compiler_params=params(1),
        cost_estimate=pl.CostEstimate(
            flops=8 * p * rows * cols, bytes_accessed=6 * rows * cols, transcendentals=0
        ),
        name="finish_residual",
    )(scales, in_hbm(x), in_hbm(s), in_hbm(lt), core, r, *parts)


def swap(value, axis, mask, size):
    return lax.ppermute(value, axis, [(i, i ^ mask) for i in range(size)])


def powers(size):
    masks = []
    mask = 1
    while mask < size:
        masks.append(mask)
        mask *= 2
    return masks


def fold(value, axis, size):
    for mask in powers(size):
        value = value + swap(value, axis, mask, size)
    return value


def gather(value, axis, size, place):
    for mask in powers(size):
        got = swap(value, axis, mask, size)
        upper = (place // mask) % 2 == 1
        value = jnp.where(
            upper, jnp.concatenate([got, value]), jnp.concatenate([value, got])
        )
    return value


def shards(n_row, n_col, x, theta_left, theta_right, query_rows, query_cols):
    rows, cols = x.shape
    p = theta_left.shape[0]
    queries = query_rows.shape[0]
    z = lax.axis_index("row")
    j = lax.axis_index("col")
    tall = min(1024, rows)
    each = rows // n_col
    share = p // n_col
    unit = max(128, cols // 8)
    if cols == 8 * unit:
        spans = [1, 2, 2, 2, 1]
        left_groups = [[0], [1], [2, 3, 4]]
    else:
        spans = [1] * (cols // unit)
        left_groups = [[c] for c in range(len(spans))]
    count = len(spans)

    row_bounds = jnp.clip(query_rows - z * rows, 0, rows)
    col_bounds = query_cols - j * cols

    segments, core_part = rights(x, theta_right, theta_left, n_col, tall)
    segments = append_core(segments, core_part, each)
    own = lax.psum_scatter(segments, "col", scatter_dimension=0, tiled=True)

    left_parts = []
    for group in left_groups:
        left_parts += lefts(
            after(theta_left, left_parts[-1] if left_parts else segments),
            x,
            sum(spans[: group[0]]),
            [spans[c] for c in group],
            unit,
            tall,
        )

    half = n_row // 2
    inward = [[(h, h + 1), (n_row - 1 - h, n_row - 2 - h)] for h in range(half - 1)]
    across = [(half - 1, half), (half, half - 1)]
    outward = [[(b, a) for a, b in pairs] for pairs in reversed(inward)]

    def hop(value, pairs):
        return lax.ppermute(value, "row", pairs)

    def send_in(value):
        for pairs in inward:
            value = value + hop(value, pairs)
        return value

    def settle(pending):
        total, got, targets = pending
        chosen = functools.reduce(jnp.logical_or, [z == t for t in targets])
        return jnp.where(chosen, got, total)

    def send_out(total):
        pending = None
        for pairs in outward:
            if pending is not None:
                total = settle(pending)
            pending = (total, hop(total, pairs), [b for _, b in pairs])
        return pending

    flight_in = {}
    for c in range(min(2, count)):
        flight_in[c] = send_in(left_parts[c])
    token = left_parts[-1]

    interval = jnp.zeros((queries, 1), F32)
    squares = jnp.zeros((), F32)
    mask_width = cols // 4
    mask_starts = list(range(0, cols, mask_width))
    last_width = left_parts[-1].shape[1]
    core_rows = share * p // last_width

    current, flight_mid, flight_out = {}, {}, {}
    lt = None
    for step in range(count + 1):
        if step < count:
            current[step] = after(flight_in[step], token)
            token = current[step]
            flight_mid[step] = hop(current[step], across)
            if step == count - 2:
                own = after(own, token)
                own_rows = own[0, :each]
                summed_right = lax.all_gather(own_rows, "col", axis=0, tiled=True)
                flight_in[count - 1] = send_in(
                    jnp.concatenate(
                        [left_parts[count - 1], own[0, each:].reshape(core_rows, last_width)]
                    )
                )
            elif step + 2 < count:
                flight_in[step + 2] = send_in(after(left_parts[step + 2], token))
        if step >= 1:
            c = step - 1
            total = after(current[c], token) + flight_mid[c]
            token = total
            flight_out[c] = send_out(total)
        if mask_starts:
            sums, square = mask_sums(
                x, after(row_bounds, token), col_bounds, mask_starts.pop(0), mask_width, tall
            )
            interval = interval + sums
            squares = squares + jnp.sum(square)
            token = sums
        elif lt is None:
            lt = after(theta_left, token).T
            token = lt
    totals = [settle(flight_out[c]) for c in range(count)]
    own_core = totals[-1][p:].reshape(share, p)
    totals[-1] = totals[-1][:p]
    core = gather(own_core, "col", n_col, j)
    t_square = sum(jnp.sum(total * total) for total in totals)

    lines = queries // 128
    scalars = jnp.stack(
        [
            squares,
            jnp.sum(own_rows * own_rows) + (t_square + jnp.sum(own_core * own_core)) / n_row,
        ]
    )
    packed = jnp.concatenate(
        [interval.reshape(lines, 128), jnp.repeat(scalars, 4)[:, None] + jnp.zeros((1, 128), F32)]
    )
    packed = fold(fold(packed, "row", n_row), "col", n_col)
    start_norm = packed[lines, 0]
    extra = packed[lines + 4, 0]
    curvature = start_norm + extra
    alpha = start_norm / curvature
    low_row, high_row = query_rows[:, 0], query_rows[:, 1]
    low_col, high_col = query_cols[:, 0], query_cols[:, 1]
    area = (high_row - low_row).astype(F32) * (high_col - low_col).astype(F32)
    answers = alpha * packed[:lines].reshape(queries) / jnp.sqrt(area)

    residual, square = finish(
        jnp.stack([extra / curvature, alpha]),
        x,
        summed_right,
        lt,
        core,
        theta_right,
        totals,
        min(256, rows),
    )
    fresh = fold(fold(jnp.full((8, 128), jnp.sum(square)), "row", n_row), "col", n_col)
    step_ratio = (fresh[0, 0] / start_norm).reshape(1)
    return (residual, step_ratio, answers)


def solution(mesh):
    return jax.shard_map(
        functools.partial(shards, mesh.shape["row"], mesh.shape["col"]),
        mesh=mesh,
        in_specs=(P("row", "col"), P(None, "row"), P(None, "col"), P(), P()),
        out_specs=(P("row", "col"), P(), P()),
        check_vma=False,
    )
```

```python
import functools

import jax
import jax.numpy as jnp
from jax import lax
from jax.experimental import pallas as pl
from jax.experimental.pallas import tpu as pltpu
from jax.sharding import PartitionSpec as P

F32 = jnp.float32
BF16 = jnp.bfloat16
VMEM_BYTES = 48 * 1024 * 1024
COST_SHARE = 0.3


def cost(macs):
    return pl.CostEstimate(
        flops=int(2 * COST_SHARE * macs), bytes_accessed=1024, transcendentals=0
    )


def params(sem_count, vmem_bytes=VMEM_BYTES):
    return pltpu.CompilerParams(
        dimension_semantics=("arbitrary",) * sem_count, vmem_limit_bytes=vmem_bytes
    )


def after(value, *earlier):
    return lax.optimization_barrier((value,) + earlier)[0]


def in_hbm(value):
    return pltpu.with_memory_space_constraint(value, pltpu.HBM)


def halves(value):
    high = value.astype(BF16)
    return high, (value - high.astype(F32)).astype(BF16)


def dot(a, b, dims=((1,), (0,))):
    return lax.dot_general(a, b, (dims, ((), ())), preferred_element_type=F32)


def rights_kernel(bit_ref, x_ref, r_ref, core_ref, sent_ref, kept_ref, square_ref):
    summed = dot(x_ref[...], r_ref[...], ((1,), (1,)))
    pairs = sent_ref.shape[0]
    share, p = core_ref.shape[1:]
    each = sent_ref.shape[1] - share
    upper = bit_ref[0] == 1
    for source, span in (
        (summed.reshape(pairs, 2, each, p), slice(0, each)),
        (core_ref[...].reshape(pairs, 2, share, p), slice(each, each + share)),
    ):
        kept_ref[:, span] = jnp.where(upper, source[:, 1], source[:, 0])
        sent_ref[:, span] = jnp.where(upper, source[:, 0], source[:, 1])
    wide = x_ref[...].astype(F32)
    square = jnp.sum(wide * wide, axis=0, keepdims=True)

    @pl.when(pl.program_id(0) == 0)
    def _():
        square_ref[...] = square

    @pl.when(pl.program_id(0) > 0)
    def _():
        square_ref[...] += square


def rights(x, r, core, bit, part, parts, groups, block):
    rows, cols = x.shape
    p = r.shape[0]
    each = rows // (parts * groups)
    share = p // (parts * groups)
    block = min(block, rows // parts)
    pairs = block // each // 2
    steps = rows // parts // block
    half = jax.ShapeDtypeStruct((groups // 2, each + share, p), F32)
    out_spec = pl.BlockSpec((pairs, each + share, p), lambda i: (i, 0, 0))
    return pl.pallas_call(
        rights_kernel,
        out_shape=[half, half, jax.ShapeDtypeStruct((1, cols), F32)],
        grid=(steps,),
        in_specs=[
            pl.BlockSpec(memory_space=pltpu.SMEM),
            pl.BlockSpec((block, cols), lambda i: (part * steps + i, 0)),
            pl.BlockSpec((p, cols), lambda i: (0, 0)),
            pl.BlockSpec((2 * pairs, share, p), lambda i: (part * steps + i, 0, 0)),
        ],
        out_specs=[out_spec, out_spec, pl.BlockSpec((1, cols), lambda i: (0, 0))],
        compiler_params=params(1),
        cost_estimate=cost(rows // parts * cols * p),
        name="right_products",
    )(bit, in_hbm(x), in_hbm(r), core.reshape(parts * groups, share, p))


def core_kernel(t_ref, r_ref, out_ref):
    right = r_ref[...]
    high, low = halves(t_ref[...])
    part = dot(high, right, ((1,), (1,))) + dot(low, right, ((1,), (1,)))

    @pl.when(pl.program_id(0) == 0)
    def _():
        out_ref[...] = part

    @pl.when(pl.program_id(0) > 0)
    def _():
        out_ref[...] += part


def core_products(t, r):
    count, cols = t.shape
    p = r.shape[0]
    width = min(1024, cols)
    return pl.pallas_call(
        core_kernel,
        out_shape=jax.ShapeDtypeStruct((count, p), F32),
        grid=(cols // width,),
        in_specs=[
            pl.BlockSpec((count, width), lambda i: (0, i)),
            pl.BlockSpec((p, width), lambda i: (0, i)),
        ],
        out_specs=pl.BlockSpec((count, p), lambda i: (0, 0)),
        compiler_params=params(1),
        cost_estimate=cost(2 * count * p * cols),
        name="core_products",
    )(in_hbm(t), in_hbm(r))


def lefts_kernel(l_ref, x_ref, out_ref):
    out_ref[...] = dot(l_ref[...], x_ref[...])


def lefts(l, x, unit):
    p, rows = l.shape
    cols = x.shape[1]
    return pl.pallas_call(
        lefts_kernel,
        out_shape=jax.ShapeDtypeStruct((p, cols), F32),
        grid=(cols // unit,),
        in_specs=[
            pl.BlockSpec((p, rows), lambda i: (0, 0)),
            pl.BlockSpec((rows, unit), lambda i: (0, i)),
        ],
        out_specs=pl.BlockSpec((p, unit), lambda i: (0, i)),
        compiler_params=params(1),
        cost_estimate=cost(p * rows * cols),
        name="left_products",
    )(in_hbm(l), in_hbm(x))


def mask_kernel(steps, col_start, rows_ref, cols_ref, x_ref, sums_ref, acc):
    step = pl.program_id(0)
    block, width = x_ref.shape
    queries = acc.shape[0]

    @pl.when(step == 0)
    def _():
        acc[...] = jnp.zeros_like(acc)

    values = x_ref[...]
    at = lax.broadcasted_iota(jnp.int32, (queries, block), 1) + step * block
    inside = (at >= rows_ref[:, 0:1]) & (at < rows_ref[:, 1:2])
    acc[...] += dot(inside.astype(F32).astype(BF16), values)

    @pl.when(step == steps - 1)
    def _():
        place = lax.broadcasted_iota(jnp.int32, (queries, width), 1) + col_start
        keep = (place >= cols_ref[:, 0:1]) & (place < cols_ref[:, 1:2])
        sums_ref[...] = jnp.sum(jnp.where(keep, acc[...], 0.0), axis=1, keepdims=True)


def mask_sums(x, row_bounds, col_bounds, start, width, block):
    rows = x.shape[0]
    queries = row_bounds.shape[0]
    steps = rows // block
    return pl.pallas_call(
        functools.partial(mask_kernel, steps, start),
        out_shape=jax.ShapeDtypeStruct((queries, 1), F32),
        grid=(steps,),
        in_specs=[
            pl.BlockSpec((queries, 2), lambda i: (0, 0)),
            pl.BlockSpec((queries, 2), lambda i: (0, 0)),
            pl.BlockSpec((block, width), lambda i: (i, start // width)),
        ],
        out_specs=pl.BlockSpec((queries, 1), lambda i: (0, 0)),
        scratch_shapes=[pltpu.VMEM((queries, width), F32)],
        compiler_params=params(1),
        cost_estimate=cost(queries * rows * width),
        name="interval_sums",
    )(row_bounds, col_bounds, in_hbm(x))


def core_spread_kernel(core_ref, r_ref, out_ref):
    high, low = halves(core_ref[...])
    right = r_ref[...]
    out_ref[...] = dot(high, right) + dot(low, right)


def core_spread(core, r):
    p, cols = r.shape
    width = min(512, cols)
    return pl.pallas_call(
        core_spread_kernel,
        out_shape=jax.ShapeDtypeStruct((p, cols), F32),
        grid=(cols // width,),
        in_specs=[
            pl.BlockSpec((p, p), lambda i: (0, 0)),
            pl.BlockSpec((p, width), lambda i: (0, i)),
        ],
        out_specs=pl.BlockSpec((p, width), lambda i: (0, i)),
        compiler_params=params(1),
        cost_estimate=cost(2 * p * p * cols),
        name="core_spread",
    )(core, in_hbm(r))


def finish_kernel(groups, bit_ref, scale_ref, x_ref, *refs):
    s_refs = refs[:4]
    lt_ref, add_ref, r_ref, t_ref, out_ref, sum_ref, both, twice = refs[4:]
    p, cols = r_ref.shape
    each = s_refs[0].shape[1]
    i = pl.program_id(0)
    width = min(512, cols)

    @pl.when(i == 0)
    def _():
        high, low = halves(t_ref[...] + add_ref[...])
        twice[:p, :] = r_ref[...]
        twice[p : 2 * p, :] = r_ref[...]
        twice[2 * p : 3 * p, :] = high
        twice[3 * p :, :] = low
        sum_ref[...] = jnp.zeros_like(sum_ref)

    upper = bit_ref[0] == 1
    early = i < groups // 2
    mine = jnp.where(early, s_refs[0][0], s_refs[2][0])
    got = jnp.where(early, s_refs[1][0], s_refs[3][0])
    for k, rows in enumerate((jnp.where(upper, got, mine), jnp.where(upper, mine, got))):
        high, low = halves(rows)
        both[k * each : (k + 1) * each, :p] = high
        both[k * each : (k + 1) * each, p : 2 * p] = low
    left = lt_ref[...]
    both[:, 2 * p : 3 * p] = left
    both[:, 3 * p :] = left
    for at in range(0, cols, width):
        span = slice(at, at + width)
        change = dot(both[...], twice[:, span])
        left_over = scale_ref[0] * x_ref[:, span].astype(F32) - scale_ref[1] * change
        out_ref[:, span] = left_over
        sum_ref[:, span] += jnp.sum(left_over * left_over, axis=0, keepdims=True)


def finish(bit, scales, x, s_parts, lt, add, r, t, groups):
    rows, cols = x.shape
    p = r.shape[0]
    each = rows // (2 * groups)
    whole = pl.BlockSpec((p, cols), lambda i: (0, 0), pipeline_mode=pl.Buffered(1))
    first = pl.BlockSpec((1, each, p), lambda i: (jnp.minimum(i, groups // 2 - 1), 0, 0))
    second = pl.BlockSpec((1, each, p), lambda i: (jnp.maximum(i - groups // 2, 0), 0, 0))
    return pl.pallas_call(
        functools.partial(finish_kernel, groups),
        out_shape=[
            jax.ShapeDtypeStruct((rows, cols), F32),
            jax.ShapeDtypeStruct((1, cols), F32),
        ],
        grid=(groups,),
        in_specs=[
            pl.BlockSpec(memory_space=pltpu.SMEM),
            pl.BlockSpec(memory_space=pltpu.SMEM),
            pl.BlockSpec((2 * each, cols), lambda i: (i, 0)),
            first,
            first,
            second,
            second,
            pl.BlockSpec((2 * each, p), lambda i: (i, 0)),
            whole,
            whole,
            whole,
        ],
        out_specs=[
            pl.BlockSpec((2 * each, cols), lambda i: (i, 0)),
            pl.BlockSpec((1, cols), lambda i: (0, 0)),
        ],
        scratch_shapes=[
            pltpu.VMEM((2 * each, 4 * p), BF16),
            pltpu.VMEM((4 * p, cols), BF16),
        ],
        compiler_params=params(1),
        cost_estimate=cost(4 * p * rows * cols),
        name="finish_residual",
    )(bit, scales, in_hbm(x), *s_parts, in_hbm(lt), add, in_hbm(r), t)


def swap(value, axis, mask, size):
    return lax.ppermute(value, axis, [(i, i ^ mask) for i in range(size)])


def powers(size):
    masks = []
    mask = 1
    while mask < size:
        masks.append(mask)
        mask *= 2
    return masks


def fold(value, axis, size):
    for mask in powers(size):
        value = value + swap(value, axis, mask, size)
    return value


def shards(n_row, n_col, x, theta_left, theta_right, query_rows, query_cols):
    rows, cols = x.shape
    p = theta_left.shape[0]
    queries = query_rows.shape[0]
    z = lax.axis_index("row")
    j = lax.axis_index("col")
    tall = min(1024, rows)
    streams = 2
    each = rows // (streams * n_col)
    share = p // (streams * n_col)
    tail = each + share
    masks = powers(n_col)
    orders = [masks, masks[:1] + masks[:0:-1]]
    bits = {mask: (j // mask) % 2 for mask in masks}
    core_bit = bits[masks[0]].astype(jnp.int32).reshape(1)
    row_bounds = jnp.clip(query_rows - z * rows, 0, rows)
    col_bounds = query_cols - j * cols

    token = theta_left

    def run(work, first, *others):
        nonlocal token
        out = work(after(first, token), *others)
        token = jax.tree.leaves(out)[0]
        return out

    def pick(value, axis, at):
        return lax.dynamic_index_in_dim(value, at, axis, False)

    partial_left = run(lambda l: lefts(l, x, min(512, cols)), theta_left)
    own_left = lax.psum_scatter(partial_left, "row", scatter_dimension=0, tiled=True)

    intervals = []
    squares = jnp.zeros((), F32)
    mask_width = cols // 4
    mask_starts = list(range(0, cols, mask_width))

    def mask_piece():
        if mask_starts:
            start = mask_starts.pop(0)
            intervals.append(
                run(lambda v: mask_sums(x, v, col_bounds, start, mask_width, tall), row_bounds)
            )

    terms = [None] * streams
    flight = [None] * streams
    left = [list(reversed(masks[1:])) for _ in range(streams)]

    def scatter_start(s, level):
        mask = orders[s][level]
        axis = left[s].index(mask)
        left[s].remove(mask)
        sent = run(
            lambda v, *rest: sum(
                (pick(term, axis, 1 - bits[mask]) for term in rest),
                pick(v, axis, 1 - bits[mask]),
            ),
            *terms[s],
        )
        terms[s] = [pick(term, axis, bits[mask]) for term in terms[s]]
        flight[s] = swap(sent, "col", mask, n_col)

    def add_start(s, level):
        terms[s].append(flight[s])
        scatter_start(s, level)

    def add_start(s, level):
        terms[s].append(flight[s])
        scatter_start(s, level)

    shape = (2,) * (len(masks) - 1)
    core = run(lambda t: core_products(t, theta_right), partial_left)
    for s in range(streams):
        sent, kept, square = run(
            lambda v: rights(x, v, core, core_bit, s, streams, n_col, tall), theta_right
        )
        squares = squares + jnp.sum(square)
        flight[s] = swap(sent, "col", masks[0], n_col).reshape(*shape, tail, p)
        terms[s] = [kept.reshape(*shape, tail, p)]
    for level in range(1, len(masks)):
        for s in range(streams):
            add_start(s, level)
        if level == 1:
            mask_piece()
            mask_piece()
    parts = []
    for s in range(streams):
        got = flight[s]
        parts.append(run(lambda v, *rest: sum(rest, v) + got, *terms[s]))

    core = jnp.concatenate([part[each:] for part in parts])
    local = [
        lambda v: sum(jnp.sum(part[:each] * part[:each]) for part in (v, parts[1])),
        lambda v: jnp.sum(own_left * own_left) + 0.0 * v[0, 0],
    ]
    total = 0.0
    for mask in powers(n_row):
        got = swap(core, "row", mask, n_row)
        if local:
            total = total + run(local.pop(0), parts[0])
        core = run(lambda v: v + got, core)
    own_left = run(lambda v: v, own_left)
    whole_left = lax.all_gather(own_left, "row", axis=0, tiled=True)
    core_square = jnp.sum(core * core)

    def widen_start(s, level):
        flight[s] = swap(parts[s], "col", orders[s][level], n_col)

    def widen(s, level):
        mask = orders[s][level]
        held = [m for m in masks if m in orders[s][level + 1 :]]
        axis = sum(1 for m in held if m > mask)
        dims = (2,) * len(held)
        other = flight[s].reshape(*dims, tail, p)
        parts[s] = run(
            lambda v: jnp.where(
                bits[mask] == 1,
                jnp.stack([other, v], axis=axis),
                jnp.stack([v, other], axis=axis),
            ),
            parts[s].reshape(*dims, tail, p),
        ).reshape(-1, tail, p)
        widen_start(s, level - 1)

    top = len(masks) - 1
    for s in range(streams):
        rows_of = jnp.concatenate([parts[s][:each], core[s * share : (s + 1) * share]])
        parts[s] = run(lambda v: v, rows_of)
        widen_start(s, top)
    sums = jnp.repeat(jnp.stack([squares, total + core_square / n_row]), 4)[:, None]
    sums = sums + jnp.zeros((1, 128), F32)
    sum_hops = [("row", m, n_row) for m in powers(n_row)] + [("col", m, n_col) for m in masks]
    sum_flight = None

    def sum_start():
        nonlocal sum_flight
        if sum_hops:
            axis, mask, size = sum_hops[0]
            sum_flight = swap(sums, axis, mask, size)

    def sum_step():
        nonlocal sums
        if sum_hops:
            sum_hops.pop(0)
            got = sum_flight
            sums = run(lambda v: v + got, sums)
            sum_start()

    sum_start()
    mask_piece()
    for level in range(top, 0, -1):
        sum_step()
        for s in range(streams):
            widen(s, level)
        mask_piece()
    while mask_starts:
        mask_piece()
    while sum_hops:
        sum_step()
    packed = sums

    pieces = []
    for s in range(streams):
        mine, other = (v.reshape(-1, tail, p)[:, each:] for v in (parts[s], flight[s]))
        pieces.append(
            jnp.where(
                bits[masks[0]] == 1,
                jnp.stack([other, mine], axis=1),
                jnp.stack([mine, other], axis=1),
            )
        )
    core = run(lambda *v: jnp.stack(v).reshape(p, p), *pieces)
    lt = run(lambda v: v.T, theta_left)
    core_add = run(lambda v: core_spread(v, theta_right), core)

    start_norm = packed[0, 0]
    extra = packed[4, 0]
    curvature = start_norm + extra
    alpha = start_norm / curvature

    residual, square = finish(
        core_bit,
        jnp.stack([extra / curvature, alpha]),
        x,
        [v.reshape(-1, tail, p) for s in range(streams) for v in (parts[s], flight[s])],
        lt,
        core_add,
        theta_right,
        whole_left,
        n_col,
    )
    lines = queries // 128
    last = jnp.concatenate(
        [sum(intervals).reshape(lines, 128), jnp.full((8, 128), jnp.sum(square))]
    )
    last = fold(fold(last, "row", n_row), "col", n_col)
    step_ratio = (last[lines, 0] / start_norm).reshape(1)
    low_row, high_row = query_rows[:, 0], query_rows[:, 1]
    low_col, high_col = query_cols[:, 0], query_cols[:, 1]
    area = (high_row - low_row).astype(F32) * (high_col - low_col).astype(F32)
    answers = alpha * last[:lines].reshape(queries) / jnp.sqrt(area)
    return (residual, step_ratio, answers)


def solution(mesh):
    return jax.shard_map(
        functools.partial(shards, mesh.shape["row"], mesh.shape["col"]),
        mesh=mesh,
        in_specs=(P("row", "col"), P(None, "row"), P(None, "col"), P(), P()),
        out_specs=(P("row", "col"), P(), P()),
        check_vma=False,
    )
```

```python
import functools

import jax
import jax.numpy as jnp
from jax import lax
from jax.experimental import pallas as pl
from jax.experimental.pallas import tpu as pltpu
from jax.sharding import PartitionSpec as P

F32 = jnp.float32
BF16 = jnp.bfloat16
F8 = jnp.float8_e4m3fn
F8_TOP = 128.0
VMEM_BYTES = 48 * 1024 * 1024
COST_SHARE = 0.3


def cost(macs):
    return pl.CostEstimate(
        flops=int(2 * COST_SHARE * macs), bytes_accessed=1024, transcendentals=0
    )


def params(sem_count, vmem_bytes=VMEM_BYTES):
    return pltpu.CompilerParams(
        dimension_semantics=("arbitrary",) * sem_count, vmem_limit_bytes=vmem_bytes
    )


def after(value, *earlier):
    return lax.optimization_barrier((value,) + earlier)[0]


def in_hbm(value):
    return pltpu.with_memory_space_constraint(value, pltpu.HBM)


def halves(value):
    high = value.astype(BF16)
    return high, (value - high.astype(F32)).astype(BF16)


def dot(a, b, dims=((1,), (0,))):
    return lax.dot_general(a, b, (dims, ((), ())), preferred_element_type=F32)


def rights_kernel(bit_ref, x_ref, r_ref, core_ref, sent_ref, kept_ref, square_ref):
    summed = dot(x_ref[...], r_ref[...], ((1,), (1,)))
    pairs = sent_ref.shape[0]
    share, p = core_ref.shape[1:]
    each = sent_ref.shape[1] - share
    upper = bit_ref[0] == 1
    for source, span in (
        (summed.reshape(pairs, 2, each, p), slice(0, each)),
        (core_ref[...].reshape(pairs, 2, share, p), slice(each, each + share)),
    ):
        kept_ref[:, span] = jnp.where(upper, source[:, 1], source[:, 0])
        sent_ref[:, span] = jnp.where(upper, source[:, 0], source[:, 1])
    wide = x_ref[...].astype(F32)
    square = jnp.sum(wide * wide, axis=0, keepdims=True)

    @pl.when(pl.program_id(0) == 0)
    def _():
        square_ref[...] = square

    @pl.when(pl.program_id(0) > 0)
    def _():
        square_ref[...] += square


def rights(x, r, core, bit, part, parts, groups, block):
    rows, cols = x.shape
    p = r.shape[0]
    each = rows // (parts * groups)
    share = p // (parts * groups)
    block = min(block, rows // parts)
    pairs = block // each // 2
    steps = rows // parts // block
    half = jax.ShapeDtypeStruct((groups // 2, each + share, p), F32)
    out_spec = pl.BlockSpec((pairs, each + share, p), lambda i: (i, 0, 0))
    return pl.pallas_call(
        rights_kernel,
        out_shape=[half, half, jax.ShapeDtypeStruct((1, cols), F32)],
        grid=(steps,),
        in_specs=[
            pl.BlockSpec(memory_space=pltpu.SMEM),
            pl.BlockSpec((block, cols), lambda i: (part * steps + i, 0)),
            pl.BlockSpec((p, cols), lambda i: (0, 0)),
            pl.BlockSpec((2 * pairs, share, p), lambda i: (part * steps + i, 0, 0)),
        ],
        out_specs=[out_spec, out_spec, pl.BlockSpec((1, cols), lambda i: (0, 0))],
        compiler_params=params(1),
        cost_estimate=cost(rows // parts * cols * p),
        name="right_products",
    )(bit, in_hbm(x), in_hbm(r), core.reshape(parts * groups, share, p))


def core_kernel(t_ref, r_ref, out_ref, most_ref):
    right = r_ref[...]
    most_ref[...] = most(right)
    high, low = halves(t_ref[...])
    part = dot(high, right, ((1,), (1,))) + dot(low, right, ((1,), (1,)))

    @pl.when(pl.program_id(0) == 0)
    def _():
        out_ref[...] = part

    @pl.when(pl.program_id(0) > 0)
    def _():
        out_ref[...] += part


def core_products(t, r):
    count, cols = t.shape
    p = r.shape[0]
    width = min(1024, cols)
    return pl.pallas_call(
        core_kernel,
        out_shape=[
            jax.ShapeDtypeStruct((count, p), F32),
            jax.ShapeDtypeStruct((1, cols), F32),
        ],
        grid=(cols // width,),
        in_specs=[
            pl.BlockSpec((count, width), lambda i: (0, i)),
            pl.BlockSpec((p, width), lambda i: (0, i)),
        ],
        out_specs=[
            pl.BlockSpec((count, p), lambda i: (0, 0)),
            pl.BlockSpec((1, width), lambda i: (0, i)),
        ],
        compiler_params=params(1),
        cost_estimate=cost(2 * count * p * cols),
        name="core_products",
    )(in_hbm(t), in_hbm(r))


def most(value):
    return jnp.max(jnp.abs(value.astype(F32)), axis=0, keepdims=True)


def lefts_kernel(l_ref, x_ref, out_ref, most_ref):
    out_ref[...] = dot(l_ref[...], x_ref[...])

    @pl.when(pl.program_id(0) == 0)
    def _():
        most_ref[...] = most(l_ref[...])


def lefts(l, x, unit):
    p, rows = l.shape
    cols = x.shape[1]
    return pl.pallas_call(
        lefts_kernel,
        out_shape=[
            jax.ShapeDtypeStruct((p, cols), F32),
            jax.ShapeDtypeStruct((1, rows), F32),
        ],
        grid=(cols // unit,),
        in_specs=[
            pl.BlockSpec((p, rows), lambda i: (0, 0)),
            pl.BlockSpec((rows, unit), lambda i: (0, i)),
        ],
        out_specs=[
            pl.BlockSpec((p, unit), lambda i: (0, i)),
            pl.BlockSpec((1, rows), lambda i: (0, 0)),
        ],
        compiler_params=params(1),
        cost_estimate=cost(p * rows * cols),
        name="left_products",
    )(in_hbm(l), in_hbm(x))


def mask_kernel(steps, col_start, rows_ref, cols_ref, x_ref, sums_ref, acc):
    step = pl.program_id(0)
    block, width = x_ref.shape
    queries = acc.shape[0]

    @pl.when(step == 0)
    def _():
        acc[...] = jnp.zeros_like(acc)

    values = x_ref[...]
    at = lax.broadcasted_iota(jnp.int32, (queries, block), 1) + step * block
    inside = (at >= rows_ref[:, 0:1]) & (at < rows_ref[:, 1:2])
    acc[...] += dot(inside.astype(F32).astype(BF16), values)

    @pl.when(step == steps - 1)
    def _():
        place = lax.broadcasted_iota(jnp.int32, (queries, width), 1) + col_start
        keep = (place >= cols_ref[:, 0:1]) & (place < cols_ref[:, 1:2])
        sums_ref[...] = jnp.sum(jnp.where(keep, acc[...], 0.0), axis=1, keepdims=True)


def mask_sums(x, row_bounds, col_bounds, start, width, block):
    rows = x.shape[0]
    queries = row_bounds.shape[0]
    steps = rows // block
    return pl.pallas_call(
        functools.partial(mask_kernel, steps, start),
        out_shape=jax.ShapeDtypeStruct((queries, 1), F32),
        grid=(steps,),
        in_specs=[
            pl.BlockSpec((queries, 2), lambda i: (0, 0)),
            pl.BlockSpec((queries, 2), lambda i: (0, 0)),
            pl.BlockSpec((block, width), lambda i: (i, start // width)),
        ],
        out_specs=pl.BlockSpec((queries, 1), lambda i: (0, 0)),
        scratch_shapes=[pltpu.VMEM((queries, width), F32)],
        compiler_params=params(1),
        cost_estimate=cost(queries * rows * width),
        name="interval_sums",
    )(row_bounds, col_bounds, in_hbm(x))


def core_spread_kernel(bit_ref, *refs):
    parts, r_ref, out_ref, high_ref, low_ref = refs[:4], *refs[4:]
    half, share, p = parts[0].shape

    @pl.when(pl.program_id(0) == 0)
    def _():
        upper = bit_ref[0] == 1
        for s in range(2):
            mine, got = parts[2 * s][...], parts[2 * s + 1][...]
            pairs = jnp.stack(
                [jnp.where(upper, got, mine), jnp.where(upper, mine, got)], axis=1
            )
            span = slice(s * 2 * half * share, (s + 1) * 2 * half * share)
            high, low = halves(pairs.reshape(2 * half * share, p))
            high_ref[span, :] = high
            low_ref[span, :] = low

    right = r_ref[...]
    out_ref[...] = dot(high_ref[...], right) + dot(low_ref[...], right)


def core_spread(bit, parts, r, each):
    p, cols = r.shape
    width = min(1024, cols)
    half, tail, _ = parts[0].shape
    share = tail - each
    return pl.pallas_call(
        core_spread_kernel,
        out_shape=jax.ShapeDtypeStruct((p, cols), F32),
        grid=(cols // width,),
        in_specs=[pl.BlockSpec(memory_space=pltpu.SMEM)]
        + [pl.BlockSpec((half, share, p), lambda i: (0, each // share, 0))] * 4
        + [pl.BlockSpec((p, width), lambda i: (0, i))],
        out_specs=pl.BlockSpec((p, width), lambda i: (0, i)),
        scratch_shapes=[pltpu.VMEM((p, p), BF16)] * 2,
        compiler_params=params(1),
        cost_estimate=cost(2 * p * p * cols),
        name="core_spread",
    )(bit, *parts, in_hbm(r))


def top_scale(largest):
    return F8_TOP / jnp.maximum(largest, 1e-25)


def finish_kernel(groups, bit_ref, scale_ref, x_ref, *refs):
    s_refs = refs[:4]
    lt_ref, add_ref, r_ref, t_ref = refs[4:8]
    out_ref, sum_ref, both, twice, low_both, low_twice, factors = refs[8:]
    p, cols = r_ref.shape
    i = pl.program_id(0)
    width = min(512, cols)

    @pl.when(i == 0)
    def _():
        whole = t_ref[...] + add_ref[...]
        high = whole.astype(BF16)
        rest = whole - high.astype(F32)
        s_most, r_scale, l_scale = scale_ref[2], scale_ref[3], scale_ref[4]
        scale = jnp.minimum(
            top_scale(s_most / 256.0) * r_scale, top_scale(jnp.max(jnp.abs(rest))) * l_scale
        )
        factors[0] = scale / r_scale
        factors[1] = scale_ref[1] / scale
        twice[:p, :] = r_ref[...]
        twice[p:, :] = high
        low_twice[:p, :] = (r_ref[...].astype(F32) * r_scale).astype(F8)
        low_twice[p:, :] = (rest * (scale / l_scale)).astype(F8)
        sum_ref[...] = jnp.zeros_like(sum_ref)

    upper = bit_ref[0] == 1
    early = i < groups // 2
    mine = jnp.where(early, s_refs[0][0], s_refs[2][0])
    got = jnp.where(early, s_refs[1][0], s_refs[3][0])
    summed = jnp.concatenate([jnp.where(upper, got, mine), jnp.where(upper, mine, got)])
    high = summed.astype(BF16)
    both[:, :p] = high
    left = lt_ref[...]
    both[:, p:] = left
    low_both[:, :p] = ((summed - high.astype(F32)) * factors[0]).astype(F8)
    low_both[:, p:] = (left.astype(F32) * scale_ref[4]).astype(F8)
    for at in range(0, cols, width):
        span = slice(at, at + width)
        left_over = (
            scale_ref[0] * x_ref[:, span].astype(F32)
            - scale_ref[1] * dot(both[...], twice[:, span])
            - factors[1] * dot(low_both[...], low_twice[:, span])
        )
        out_ref[:, span] = left_over
        sum_ref[:, span] += jnp.sum(left_over * left_over, axis=0, keepdims=True)


def finish(bit, scales, x, s_parts, lt, add, r, t, groups):
    rows, cols = x.shape
    p = r.shape[0]
    each = rows // (2 * groups)
    whole = pl.BlockSpec((p, cols), lambda i: (0, 0), pipeline_mode=pl.Buffered(1))
    first = pl.BlockSpec((1, each, p), lambda i: (jnp.minimum(i, groups // 2 - 1), 0, 0))
    second = pl.BlockSpec((1, each, p), lambda i: (jnp.maximum(i - groups // 2, 0), 0, 0))
    return pl.pallas_call(
        functools.partial(finish_kernel, groups),
        out_shape=[
            jax.ShapeDtypeStruct((rows, cols), F32),
            jax.ShapeDtypeStruct((1, cols), F32),
        ],
        grid=(groups,),
        in_specs=[
            pl.BlockSpec(memory_space=pltpu.SMEM),
            pl.BlockSpec(memory_space=pltpu.SMEM),
            pl.BlockSpec((2 * each, cols), lambda i: (i, 0)),
            first,
            first,
            second,
            second,
            pl.BlockSpec((2 * each, p), lambda i: (i, 0)),
            whole,
            whole,
            whole,
        ],
        out_specs=[
            pl.BlockSpec((2 * each, cols), lambda i: (i, 0)),
            pl.BlockSpec((1, cols), lambda i: (0, 0)),
        ],
        scratch_shapes=[
            pltpu.VMEM((2 * each, 2 * p), BF16),
            pltpu.VMEM((2 * p, cols), BF16),
            pltpu.VMEM((2 * each, 2 * p), F8),
            pltpu.VMEM((2 * p, cols), F8),
            pltpu.SMEM((2,), F32),
        ],
        compiler_params=params(1),
        cost_estimate=cost(4 * p * rows * cols),
        name="finish_residual",
    )(bit, scales, in_hbm(x), *s_parts, in_hbm(lt), in_hbm(add), in_hbm(r), in_hbm(t))


def swap(value, axis, mask, size):
    return lax.ppermute(value, axis, [(i, i ^ mask) for i in range(size)])


def powers(size):
    masks = []
    mask = 1
    while mask < size:
        masks.append(mask)
        mask *= 2
    return masks


def fold(value, axis, size):
    for mask in powers(size):
        value = value + swap(value, axis, mask, size)
    return value


def shards(n_row, n_col, x, theta_left, theta_right, query_rows, query_cols):
    rows, cols = x.shape
    p = theta_left.shape[0]
    queries = query_rows.shape[0]
    z = lax.axis_index("row")
    j = lax.axis_index("col")
    tall = min(1024, rows)
    streams = 2
    each = rows // (streams * n_col)
    share = p // (streams * n_col)
    tail = each + share
    masks = powers(n_col)
    orders = [masks, masks[:1] + masks[:0:-1]]
    bits = {mask: (j // mask) % 2 for mask in masks}
    core_bit = bits[masks[0]].astype(jnp.int32).reshape(1)
    row_bounds = jnp.clip(query_rows - z * rows, 0, rows)
    col_bounds = query_cols - j * cols

    token = theta_left

    def run(work, first, *others):
        nonlocal token
        out = work(after(first, token), *others)
        token = jax.tree.leaves(out)[0]
        return out

    def pick(value, axis, at):
        return lax.dynamic_index_in_dim(value, at, axis, False)

    partial_left, l_most = run(lambda l: lefts(l, x, min(512, cols)), theta_left)
    own_left = lax.psum_scatter(partial_left, "row", scatter_dimension=0, tiled=True)

    intervals = []
    squares = jnp.zeros((), F32)
    mask_width = cols // 4
    mask_starts = list(range(0, cols, mask_width))

    def mask_piece():
        if mask_starts:
            start = mask_starts.pop(0)
            intervals.append(
                run(lambda v: mask_sums(x, v, col_bounds, start, mask_width, tall), row_bounds)
            )

    terms = [None] * streams
    flight = [None] * streams
    left = [list(reversed(masks[1:])) for _ in range(streams)]

    def scatter_start(s, level):
        mask = orders[s][level]
        axis = left[s].index(mask)
        left[s].remove(mask)
        sent = run(
            lambda v, *rest: sum(
                (pick(term, axis, 1 - bits[mask]) for term in rest),
                pick(v, axis, 1 - bits[mask]),
            ),
            *terms[s],
        )
        terms[s] = [pick(term, axis, bits[mask]) for term in terms[s]]
        flight[s] = swap(sent, "col", mask, n_col)

    def add_start(s, level):
        terms[s].append(flight[s])
        scatter_start(s, level)

    def add_start(s, level):
        terms[s].append(flight[s])
        scatter_start(s, level)

    shape = (2,) * (len(masks) - 1)
    core, r_most = run(lambda t: core_products(t, theta_right), partial_left)
    for s in range(streams):
        sent, kept, square = run(
            lambda v: rights(x, v, core, core_bit, s, streams, n_col, tall), theta_right
        )
        squares = squares + jnp.sum(square)
        flight[s] = swap(sent, "col", masks[0], n_col).reshape(*shape, tail, p)
        terms[s] = [kept.reshape(*shape, tail, p)]
    for level in range(1, len(masks)):
        for s in range(streams):
            add_start(s, level)
        if level == 1:
            mask_piece()
            mask_piece()
    parts = []
    for s in range(streams):
        got = flight[s]
        parts.append(run(lambda v, *rest: sum(rest, v) + got, *terms[s]))

    own_left = run(lambda v: v, own_left)
    whole_left = lax.all_gather(own_left, "row", axis=0, tiled=True)
    top = len(masks) - 1
    for s in range(streams):
        flight[s] = swap(run(lambda v: v[:each], parts[s]), "col", orders[s][top], n_col)

    core = jnp.concatenate([part[each:] for part in parts])
    total = 0.0
    s_most = jnp.maximum(*[jnp.max(jnp.abs(part[:each])) for part in parts])
    local = [
        lambda v: sum(jnp.sum(part[:each] * part[:each]) for part in (v, parts[1])),
        lambda v: jnp.sum(own_left * own_left) + 0.0 * v[0, 0],
    ]
    for mask in powers(n_row):
        got = swap(core, "row", mask, n_row)
        if local:
            total = total + run(local.pop(0), parts[0])
        if not local:
            mask_piece()
        core = run(lambda v: v + got, core)
    core_square = jnp.sum(core * core)
    core_parts = jnp.split(core, streams)
    core_flight = [
        swap(core_parts[s], "col", orders[s][top], n_col) for s in range(streams)
    ]

    def widen_start(s, level):
        flight[s] = swap(parts[s], "col", orders[s][level], n_col)

    def widen(s, level):
        mask = orders[s][level]
        held = [m for m in masks if m in orders[s][level + 1 :]]
        axis = sum(1 for m in held if m > mask)
        dims = (2,) * len(held)
        if level == top:
            flight[s] = jnp.concatenate([flight[s], core_flight[s]])
            parts[s] = jnp.concatenate([parts[s][:each], core_parts[s]])
        other = flight[s].reshape(*dims, tail, p)
        parts[s] = run(
            lambda v: jnp.where(
                bits[mask] == 1,
                jnp.stack([other, v], axis=axis),
                jnp.stack([v, other], axis=axis),
            ),
            parts[s].reshape(*dims, tail, p),
        ).reshape(-1, tail, p)
        widen_start(s, level - 1)

    lane = lax.broadcasted_iota(jnp.int32, (8, 128), 0)
    sums = jnp.where(
        lane < 3, squares, jnp.where(lane < 6, total + core_square / n_row, s_most)
    )
    sum_hops = [("row", m, n_row) for m in powers(n_row)] + [("col", m, n_col) for m in masks]
    sum_flight = None

    def sum_start():
        nonlocal sum_flight
        if sum_hops:
            axis, mask, size = sum_hops[0]
            sum_flight = swap(sums, axis, mask, size)

    def sum_step():
        nonlocal sums
        if sum_hops:
            sum_hops.pop(0)
            got = sum_flight
            sums = run(lambda v: jnp.where(lane < 6, v + got, jnp.maximum(v, got)), sums)
            sum_start()

    sum_start()
    lt = run(lambda v: v.T, theta_left)
    l_scale = top_scale(jnp.max(l_most))
    r_scale = top_scale(jnp.max(r_most))
    for level in range(top, 0, -1):
        for s in range(streams):
            widen(s, level)
        sum_step()
        if level == top:
            while mask_starts:
                mask_piece()
            sum_step()
            sum_step()
            sum_step()
    while sum_hops:
        sum_step()
    packed = sums

    s_parts = [v.reshape(-1, tail, p) for s in range(streams) for v in (parts[s], flight[s])]
    core_add = run(lambda v: core_spread(core_bit, [v] + s_parts[1:], theta_right, each), s_parts[0])

    start_norm = packed[0, 0]
    extra = packed[3, 0]
    curvature = start_norm + extra
    alpha = start_norm / curvature

    residual, square = finish(
        core_bit,
        jnp.stack([extra / curvature, alpha, packed[6, 0], r_scale, l_scale]),
        x,
        s_parts,
        lt,
        core_add,
        theta_right,
        whole_left,
        n_col,
    )
    lines = queries // 128
    last = jnp.concatenate(
        [sum(intervals).reshape(lines, 128), jnp.full((8, 128), jnp.sum(square))]
    )
    last = fold(fold(last, "row", n_row), "col", n_col)
    step_ratio = (last[lines, 0] / start_norm).reshape(1)
    low_row, high_row = query_rows[:, 0], query_rows[:, 1]
    low_col, high_col = query_cols[:, 0], query_cols[:, 1]
    area = (high_row - low_row).astype(F32) * (high_col - low_col).astype(F32)
    answers = alpha * last[:lines].reshape(queries) / jnp.sqrt(area)
    return (residual, step_ratio, answers)


def solution(mesh):
    return jax.shard_map(
        functools.partial(shards, mesh.shape["row"], mesh.shape["col"]),
        mesh=mesh,
        in_specs=(P("row", "col"), P(None, "row"), P(None, "col"), P(), P()),
        out_specs=(P("row", "col"), P(), P()),
        check_vma=False,
    )
```

```python
import functools

import jax
import jax.numpy as jnp
from jax import lax
from jax.experimental import pallas as pl
from jax.experimental.pallas import tpu as pltpu
from jax.sharding import PartitionSpec as P

F32 = jnp.float32
BF16 = jnp.bfloat16
F8 = jnp.float8_e4m3fn
F8_TOP = 128.0
VMEM_BYTES = 48 * 1024 * 1024
COST_SHARE = 0.3


def cost(macs):
    return pl.CostEstimate(
        flops=int(2 * COST_SHARE * macs), bytes_accessed=1024, transcendentals=0
    )


def params(sem_count, vmem_bytes=VMEM_BYTES):
    return pltpu.CompilerParams(
        dimension_semantics=("arbitrary",) * sem_count, vmem_limit_bytes=vmem_bytes
    )


def after(value, *earlier):
    return lax.optimization_barrier((value,) + earlier)[0]


def in_hbm(value):
    return pltpu.with_memory_space_constraint(value, pltpu.HBM)


def hbm_shape(shape):
    return pltpu.HBM(shape, F32)


def halves(value):
    high = value.astype(BF16)
    return high, (value - high.astype(F32)).astype(BF16)


def dot(a, b, dims=((1,), (0,))):
    return lax.dot_general(a, b, (dims, ((), ())), preferred_element_type=F32)


def rights_kernel(bit_ref, x_ref, r_ref, core_ref, sent_ref, kept_ref, square_ref):
    summed = dot(x_ref[...], r_ref[...], ((1,), (1,)))
    pairs = sent_ref.shape[0]
    share, p = core_ref.shape[1:]
    each = sent_ref.shape[1] - share
    upper = bit_ref[0] == 1
    for source, span in (
        (summed.reshape(pairs, 2, each, p), slice(0, each)),
        (core_ref[...].reshape(pairs, 2, share, p), slice(each, each + share)),
    ):
        kept_ref[:, span] = jnp.where(upper, source[:, 1], source[:, 0])
        sent_ref[:, span] = jnp.where(upper, source[:, 0], source[:, 1])
    wide = x_ref[...].astype(F32)
    square = jnp.sum(wide * wide, axis=0, keepdims=True)

    @pl.when(pl.program_id(0) == 0)
    def _():
        square_ref[...] = square

    @pl.when(pl.program_id(0) > 0)
    def _():
        square_ref[...] += square


def rights(x, r, core, bit, part, parts, groups, block):
    rows, cols = x.shape
    p = r.shape[0]
    each = rows // (parts * groups)
    share = p // (parts * groups)
    block = min(block, rows // parts)
    pairs = block // each // 2
    steps = rows // parts // block
    half = jax.ShapeDtypeStruct((groups // 2, each + share, p), F32)
    out_spec = pl.BlockSpec((pairs, each + share, p), lambda i: (i, 0, 0))
    return pl.pallas_call(
        rights_kernel,
        out_shape=[half, half, jax.ShapeDtypeStruct((1, cols), F32)],
        grid=(steps,),
        in_specs=[
            pl.BlockSpec(memory_space=pltpu.SMEM),
            pl.BlockSpec((block, cols), lambda i: (part * steps + i, 0)),
            pl.BlockSpec((p, cols), lambda i: (0, 0)),
            pl.BlockSpec((2 * pairs, share, p), lambda i: (part * steps + i, 0, 0)),
        ],
        out_specs=[out_spec, out_spec, pl.BlockSpec((1, cols), lambda i: (0, 0))],
        compiler_params=params(1),
        cost_estimate=cost(rows // parts * cols * p),
        name="right_products",
    )(bit, in_hbm(x), in_hbm(r), core.reshape(parts * groups, share, p))


def core_kernel(t_ref, r_ref, out_ref, most_ref):
    right = r_ref[...]
    most_ref[...] = most(right)
    high, low = halves(t_ref[...])
    part = dot(high, right, ((1,), (1,))) + dot(low, right, ((1,), (1,)))

    @pl.when(pl.program_id(0) == 0)
    def _():
        out_ref[...] = part

    @pl.when(pl.program_id(0) > 0)
    def _():
        out_ref[...] += part


def core_products(t, r):
    count, cols = t.shape
    p = r.shape[0]
    width = min(1024, cols)
    return pl.pallas_call(
        core_kernel,
        out_shape=[
            jax.ShapeDtypeStruct((count, p), F32),
            jax.ShapeDtypeStruct((1, cols), F32),
        ],
        grid=(cols // width,),
        in_specs=[
            pl.BlockSpec((count, width), lambda i: (0, i)),
            pl.BlockSpec((p, width), lambda i: (0, i)),
        ],
        out_specs=[
            pl.BlockSpec((count, p), lambda i: (0, 0)),
            pl.BlockSpec((1, width), lambda i: (0, i)),
        ],
        compiler_params=params(1),
        cost_estimate=cost(2 * count * p * cols),
        name="core_products",
    )(in_hbm(t), in_hbm(r))


def most(value):
    return jnp.max(jnp.abs(value.astype(F32)), axis=0, keepdims=True)


def lefts_kernel(l_ref, x_ref, out_ref, most_ref):
    out_ref[...] = dot(l_ref[...], x_ref[...])

    @pl.when(pl.program_id(0) == 0)
    def _():
        most_ref[...] = most(l_ref[...])


def lefts(l, x, unit):
    p, rows = l.shape
    cols = x.shape[1]
    return pl.pallas_call(
        lefts_kernel,
        out_shape=[hbm_shape((p, cols)), jax.ShapeDtypeStruct((1, rows), F32)],
        grid=(cols // unit,),
        in_specs=[
            pl.BlockSpec((p, rows), lambda i: (0, 0)),
            pl.BlockSpec((rows, unit), lambda i: (0, i)),
        ],
        out_specs=[
            pl.BlockSpec((p, unit), lambda i: (0, i)),
            pl.BlockSpec((1, rows), lambda i: (0, 0)),
        ],
        compiler_params=params(1),
        cost_estimate=cost(p * rows * cols),
        name="left_products",
    )(in_hbm(l), in_hbm(x))


def mask_kernel(steps, col_start, rows_ref, cols_ref, x_ref, sums_ref, acc):
    step = pl.program_id(0)
    block, width = x_ref.shape
    queries = acc.shape[0]

    @pl.when(step == 0)
    def _():
        acc[...] = jnp.zeros_like(acc)

    values = x_ref[...]
    at = lax.broadcasted_iota(jnp.int32, (queries, block), 1) + step * block
    inside = (at >= rows_ref[:, 0:1]) & (at < rows_ref[:, 1:2])
    acc[...] += dot(inside.astype(F32).astype(BF16), values)

    @pl.when(step == steps - 1)
    def _():
        place = lax.broadcasted_iota(jnp.int32, (queries, width), 1) + col_start
        keep = (place >= cols_ref[:, 0:1]) & (place < cols_ref[:, 1:2])
        sums_ref[...] = jnp.sum(jnp.where(keep, acc[...], 0.0), axis=1, keepdims=True)


def mask_sums(x, row_bounds, col_bounds, start, width, block):
    rows = x.shape[0]
    queries = row_bounds.shape[0]
    steps = rows // block
    return pl.pallas_call(
        functools.partial(mask_kernel, steps, start),
        out_shape=jax.ShapeDtypeStruct((queries, 1), F32),
        grid=(steps,),
        in_specs=[
            pl.BlockSpec((queries, 2), lambda i: (0, 0)),
            pl.BlockSpec((queries, 2), lambda i: (0, 0)),
            pl.BlockSpec((block, width), lambda i: (i, start // width)),
        ],
        out_specs=pl.BlockSpec((queries, 1), lambda i: (0, 0)),
        scratch_shapes=[pltpu.VMEM((queries, width), F32)],
        compiler_params=params(1),
        cost_estimate=cost(queries * rows * width),
        name="interval_sums",
    )(row_bounds, col_bounds, in_hbm(x))


def core_spread_kernel(bit_ref, *refs):
    parts, r_ref, out_ref, square_ref, high_ref, low_ref = refs[:4], *refs[4:]
    half, share, p = parts[0].shape

    @pl.when(pl.program_id(0) == 0)
    def _():
        upper = bit_ref[0] == 1
        square_ref[...] = jnp.zeros_like(square_ref)
        for s in range(2):
            mine, got = parts[2 * s][...], parts[2 * s + 1][...]
            pairs = jnp.stack(
                [jnp.where(upper, got, mine), jnp.where(upper, mine, got)], axis=1
            )
            span = slice(s * 2 * half * share, (s + 1) * 2 * half * share)
            square_ref[...] += jnp.sum(pairs * pairs)
            high, low = halves(pairs.reshape(2 * half * share, p))
            high_ref[span, :] = high
            low_ref[span, :] = low

    right = r_ref[...]
    out_ref[...] = dot(high_ref[...], right) + dot(low_ref[...], right)


def core_spread(bit, parts, r, each):
    p, cols = r.shape
    width = min(1024, cols)
    half, tail, _ = parts[0].shape
    share = tail - each
    return pl.pallas_call(
        core_spread_kernel,
        out_shape=[
            hbm_shape((p, cols)),
            jax.ShapeDtypeStruct((1, 128), F32),
        ],
        grid=(cols // width,),
        in_specs=[pl.BlockSpec(memory_space=pltpu.SMEM)]
        + [pl.BlockSpec((half, share, p), lambda i: (0, each // share, 0))] * 4
        + [pl.BlockSpec((p, width), lambda i: (0, i))],
        out_specs=[
            pl.BlockSpec((p, width), lambda i: (0, i)),
            pl.BlockSpec((1, 128), lambda i: (0, 0)),
        ],
        scratch_shapes=[pltpu.VMEM((p, p), BF16)] * 2,
        compiler_params=params(1),
        cost_estimate=cost(2 * p * p * cols),
        name="core_spread",
    )(bit, *[in_hbm(v) for v in parts], in_hbm(r))


def top_scale(largest):
    return F8_TOP / jnp.maximum(largest, 1e-25)


def finish_kernel(groups, bit_ref, packed_ref, square_ref, l_ref, rm_ref, x_ref, *refs):
    s_refs = refs[:4]
    lt_ref, add_ref, r_ref, t_ref = refs[4:8]
    out_ref, total_ref, sum_ref, both, twice, low_both, low_twice, factors = refs[8:]
    p, cols = r_ref.shape
    i = pl.program_id(0)
    width = min(512, cols)

    @pl.when(i == 0)
    def _():
        whole = t_ref[...] + add_ref[...]
        high = whole.astype(BF16)
        rest = whole - high.astype(F32)
        start_norm = jnp.max(packed_ref[0:1, :])
        extra = jnp.max(packed_ref[3:4, :]) + jnp.max(square_ref[...])
        alpha = start_norm / (start_norm + extra)
        s_most = jnp.max(packed_ref[6:7, :])
        l_scale = top_scale(jnp.max(l_ref[...]))
        r_scale = top_scale(jnp.max(rm_ref[...]))
        scale = jnp.minimum(
            top_scale(s_most / 256.0) * r_scale, top_scale(jnp.max(jnp.abs(rest))) * l_scale
        )
        factors[0] = scale / r_scale
        factors[1] = alpha / scale
        factors[2] = alpha
        factors[3] = extra / (start_norm + extra)
        factors[4] = l_scale
        twice[:p, :] = r_ref[...]
        twice[p:, :] = high
        low_twice[:p, :] = (r_ref[...].astype(F32) * r_scale).astype(F8)
        low_twice[p:, :] = (rest * (scale / l_scale)).astype(F8)
        sum_ref[...] = jnp.zeros_like(sum_ref)

    upper = bit_ref[0] == 1
    early = i < groups // 2
    mine = jnp.where(early, s_refs[0][0], s_refs[2][0])
    got = jnp.where(early, s_refs[1][0], s_refs[3][0])
    summed = jnp.concatenate([jnp.where(upper, got, mine), jnp.where(upper, mine, got)])
    high = summed.astype(BF16)
    both[:, :p] = high
    left = lt_ref[...]
    both[:, p:] = left
    low_both[:, :p] = ((summed - high.astype(F32)) * factors[0]).astype(F8)
    low_both[:, p:] = (left.astype(F32) * factors[4]).astype(F8)
    for at in range(0, cols, width):
        span = slice(at, at + width)
        left_over = (
            factors[3] * x_ref[:, span].astype(F32)
            - factors[2] * dot(both[...], twice[:, span])
            - factors[1] * dot(low_both[...], low_twice[:, span])
        )
        out_ref[:, span] = left_over
        sum_ref[:, span] += jnp.sum(left_over * left_over, axis=0, keepdims=True)

    @pl.when(i == groups - 1)
    def _():
        total_ref[...] = jnp.full(total_ref.shape, jnp.sum(sum_ref[...]))


def finish(bit, packed, square, l_most, r_most, x, s_parts, lt, add, r, t, groups):
    rows, cols = x.shape
    p = r.shape[0]
    each = rows // (2 * groups)
    whole = pl.BlockSpec((p, cols), lambda i: (0, 0), pipeline_mode=pl.Buffered(1))
    first = pl.BlockSpec((1, each, p), lambda i: (jnp.minimum(i, groups // 2 - 1), 0, 0))
    second = pl.BlockSpec((1, each, p), lambda i: (jnp.maximum(i - groups // 2, 0), 0, 0))
    return pl.pallas_call(
        functools.partial(finish_kernel, groups),
        out_shape=[
            jax.ShapeDtypeStruct((rows, cols), F32),
            jax.ShapeDtypeStruct((8, 128), F32),
        ],
        grid=(groups,),
        in_specs=[
            pl.BlockSpec(memory_space=pltpu.SMEM),
            pl.BlockSpec((8, 128), lambda i: (0, 0)),
            pl.BlockSpec((1, 128), lambda i: (0, 0)),
            pl.BlockSpec((1, rows), lambda i: (0, 0)),
            pl.BlockSpec((1, cols), lambda i: (0, 0)),
            pl.BlockSpec((2 * each, cols), lambda i: (i, 0)),
            first,
            first,
            second,
            second,
            pl.BlockSpec((2 * each, p), lambda i: (i, 0)),
            whole,
            whole,
            whole,
        ],
        out_specs=[
            pl.BlockSpec((2 * each, cols), lambda i: (i, 0)),
            pl.BlockSpec((8, 128), lambda i: (0, 0)),
        ],
        scratch_shapes=[
            pltpu.VMEM((1, cols), F32),
            pltpu.VMEM((2 * each, 2 * p), BF16),
            pltpu.VMEM((2 * p, cols), BF16),
            pltpu.VMEM((2 * each, 2 * p), F8),
            pltpu.VMEM((2 * p, cols), F8),
            pltpu.SMEM((5,), F32),
        ],
        compiler_params=params(1),
        cost_estimate=cost(4 * p * rows * cols),
        name="finish_residual",
    )(bit, packed, square, l_most, r_most, in_hbm(x), *[in_hbm(v) for v in s_parts], in_hbm(lt), in_hbm(add), in_hbm(r), in_hbm(t))


def swap(value, axis, mask, size):
    return lax.ppermute(value, axis, [(i, i ^ mask) for i in range(size)])


def powers(size):
    masks = []
    mask = 1
    while mask < size:
        masks.append(mask)
        mask *= 2
    return masks


def fold(value, axis, size):
    for mask in powers(size):
        value = value + swap(value, axis, mask, size)
    return value


def shards(n_row, n_col, x, theta_left, theta_right, query_rows, query_cols):
    rows, cols = x.shape
    p = theta_left.shape[0]
    queries = query_rows.shape[0]
    z = lax.axis_index("row")
    j = lax.axis_index("col")
    tall = min(1024, rows)
    streams = 2
    each = rows // (streams * n_col)
    share = p // (streams * n_col)
    tail = each + share
    masks = powers(n_col)
    orders = [masks, masks[:1] + masks[:0:-1]]
    bits = {mask: (j // mask) % 2 for mask in masks}
    core_bit = bits[masks[0]].astype(jnp.int32).reshape(1)
    row_bounds = jnp.clip(query_rows - z * rows, 0, rows)
    col_bounds = query_cols - j * cols

    token = theta_left

    def run(work, first, *others):
        nonlocal token
        out = work(after(first, token), *others)
        token = jax.tree.leaves(out)[0]
        return out

    def pick(value, axis, at):
        return lax.dynamic_index_in_dim(value, at, axis, False)

    partial_left, l_most = run(lambda l: lefts(l, x, min(512, cols)), theta_left)
    own_left = lax.psum_scatter(partial_left, "row", scatter_dimension=0, tiled=True)

    intervals = []
    squares = jnp.zeros((), F32)
    mask_width = cols // 4
    mask_starts = list(range(0, cols, mask_width))

    def mask_piece():
        if mask_starts:
            start = mask_starts.pop(0)
            intervals.append(
                run(lambda v: mask_sums(x, v, col_bounds, start, mask_width, tall), row_bounds)
            )

    terms = [None] * streams
    flight = [None] * streams
    left = [list(reversed(masks[1:])) for _ in range(streams)]

    def scatter_start(s, level):
        mask = orders[s][level]
        axis = left[s].index(mask)
        left[s].remove(mask)
        sent = run(
            lambda v, *rest: sum(
                (pick(term, axis, 1 - bits[mask]) for term in rest),
                pick(v, axis, 1 - bits[mask]),
            ),
            *terms[s],
        )
        terms[s] = [pick(term, axis, bits[mask]) for term in terms[s]]
        flight[s] = swap(sent, "col", mask, n_col)

    def add_start(s, level):
        terms[s].append(flight[s])
        scatter_start(s, level)

    def add_start(s, level):
        terms[s].append(flight[s])
        scatter_start(s, level)

    shape = (2,) * (len(masks) - 1)
    core, r_most = run(lambda t: core_products(t, theta_right), partial_left)
    for s in range(streams):
        sent, kept, square = run(
            lambda v: rights(x, v, core, core_bit, s, streams, n_col, tall), theta_right
        )
        squares = squares + jnp.sum(square)
        flight[s] = swap(sent, "col", masks[0], n_col).reshape(*shape, tail, p)
        terms[s] = [kept.reshape(*shape, tail, p)]
    for level in range(1, len(masks)):
        for s in range(streams):
            add_start(s, level)
        if level == 1:
            mask_piece()
            mask_piece()
    parts = []
    for s in range(streams):
        got = flight[s]
        parts.append(run(lambda v, *rest: sum(rest, v) + got, *terms[s]))

    own_left = run(lambda v: v, own_left)
    whole_left = lax.all_gather(own_left, "row", axis=0, tiled=True)
    top = len(masks) - 1
    for s in range(streams):
        flight[s] = swap(run(lambda v: v[:each], parts[s]), "col", orders[s][top], n_col)

    total = run(
        lambda v: sum(jnp.sum(part[:each] * part[:each]) for part in (v, parts[1])), parts[0]
    )
    total = total + run(lambda v: jnp.sum(v * v), own_left)
    s_most = run(
        lambda v: jnp.maximum(*[jnp.max(jnp.abs(part[:each])) for part in (v, parts[1])]),
        parts[0],
    )
    lane = lax.broadcasted_iota(jnp.int32, (8, 128), 0)
    sums = jnp.where(lane < 3, squares, jnp.where(lane < 6, total, s_most))
    sum_hops = [("row", m, n_row) for m in powers(n_row)] + [("col", m, n_col) for m in masks]
    sum_flight = None

    def sum_start():
        nonlocal sum_flight
        if sum_hops:
            axis, mask, size = sum_hops[0]
            sum_flight = swap(sums, axis, mask, size)

    def sum_step():
        nonlocal sums
        if sum_hops:
            sum_hops.pop(0)
            got = sum_flight
            sums = run(lambda v: jnp.where(lane < 6, v + got, jnp.maximum(v, got)), sums)
            sum_start()

    core = jnp.concatenate([part[each:] for part in parts])
    for k, mask in enumerate(powers(n_row)):
        got = swap(core, "row", mask, n_row)
        if k == 0:
            sum_start()
        else:
            mask_piece()
        core = run(lambda v: v + got, core)
        sum_step()
    core_parts = jnp.split(core, streams)
    core_flight = [
        swap(core_parts[s], "col", orders[s][top], n_col) for s in range(streams)
    ]

    def widen_start(s, level):
        flight[s] = swap(parts[s], "col", orders[s][level], n_col)

    def widen(s, level):
        mask = orders[s][level]
        held = [m for m in masks if m in orders[s][level + 1 :]]
        axis = sum(1 for m in held if m > mask)
        dims = (2,) * len(held)
        if level == top:
            flight[s] = jnp.concatenate([flight[s], core_flight[s]])
            parts[s] = jnp.concatenate([parts[s][:each], core_parts[s]])
        other = flight[s].reshape(*dims, tail, p)
        parts[s] = run(
            lambda v: jnp.where(
                bits[mask] == 1,
                jnp.stack([other, v], axis=axis),
                jnp.stack([v, other], axis=axis),
            ),
            parts[s].reshape(*dims, tail, p),
        ).reshape(-1, tail, p)
        widen_start(s, level - 1)

    for level in range(top, 0, -1):
        if level == top:
            sum_step()
        for s in range(streams):
            widen(s, level)
        if level == top:
            while mask_starts:
                mask_piece()
            lt = run(lambda v: v.T, theta_left)
            while sum_hops:
                sum_step()
    packed = sums

    s_parts = [v.reshape(-1, tail, p) for s in range(streams) for v in (parts[s], flight[s])]
    core_add, core_square = run(
        lambda v: core_spread(core_bit, [v] + s_parts[1:], theta_right, each), s_parts[0]
    )

    start_norm = packed[0, 0]
    alpha = start_norm / (start_norm + packed[3, 0] + core_square[0, 0])
    low_row, high_row = query_rows[:, 0], query_rows[:, 1]
    low_col, high_col = query_cols[:, 0], query_cols[:, 1]
    area = (high_row - low_row).astype(F32) * (high_col - low_col).astype(F32)
    lines = queries // 128
    scale = run(lambda v: (alpha / jnp.sqrt(v)).reshape(lines, 128), area)
    back = run(lambda v: jnp.broadcast_to(1.0 / v, (8, 128)), start_norm)

    residual, square = finish(
        core_bit,
        after(packed, scale, back),
        core_square,
        l_most,
        r_most,
        x,
        s_parts,
        lt,
        core_add,
        theta_right,
        whole_left,
        n_col,
    )
    last = jnp.concatenate([sum(intervals).reshape(lines, 128), square])
    last = fold(fold(last, "row", n_row), "col", n_col) * jnp.concatenate([scale, back])
    return (residual, last[lines, :1], last[:lines].reshape(queries))


def solution(mesh):
    return jax.shard_map(
        functools.partial(shards, mesh.shape["row"], mesh.shape["col"]),
        mesh=mesh,
        in_specs=(P("row", "col"), P(None, "row"), P(None, "col"), P(), P()),
        out_specs=(P("row", "col"), P(), P()),
        check_vma=False,
    )
```
